512 devices in a mesh: row: 16 (over z_lo, x), col: 32 (over y, z_hi, core).
Axes of the slice: x: 4, y: 8, z: 8 (z_hi: 2, z_lo: 4; z = z_hi * 4 + z_lo), core: 2. Of those that a mesh axis runs over, the one named last changes fastest.
Arguments:
- inputs: bfloat16 [512, 6144], P('row'), may hold values from -6 to 6
- cotangent: bfloat16 [512, 24576], P('row', 'col'), may hold values from -1.1953125 to 1.1953125
- gate_weight: bfloat16 [6144, 24576], P('row', 'col'), may hold values from -0.078125 to 0.078125
- up_weight: bfloat16 [6144, 24576], P('row', 'col'), may hold values from -0.078125 to 0.078125
Outputs:
- input_grad: bfloat16 [512, 6144], P('col', 'row')
- gate_grad: bfloat16 [6144, 24576], P('row', 'col')
- up_grad: bfloat16 [6144, 24576], P('row', 'col')
The draws below stay inside these ranges and needn't reach their ends.
All inputs are finite; a program needn't handle non-finite values.
Results may differ from the reference program's by a relative error of at most 0.005.
Values may be sent and summed in bfloat16 or wider, within the bound.
No kernel may reach another device: no remote copies, remote signals or barrier semaphores. Data moves between devices by JAX's collectives and lax.ppermute only.
A program may use at most 64 MiB of HBM per device.

```python
import jax
import jax.numpy as jnp

D = 6144
FF = 24576
TOKENS = 512


def block_scale(own_key, shape, pieces, low, high):
    gain, own = 1.0, jax.random.fold_in(own_key, 6)
    for dim, shards_of in pieces:
        draws = jnp.exp(jax.random.uniform(jax.random.fold_in(own, dim), (shards_of,), jnp.float32, low / len(pieces), high / len(pieces)))
        gain = gain * jnp.repeat(draws, shape[dim] // shards_of).reshape([-1 if axis == dim else 1 for axis in range(len(shape))])
    return gain


def scatter_about(rng, shape, spread, bound, shards=(), dtype=jnp.bfloat16):
    values = jax.random.normal(rng, shape, jnp.float32) * spread
    if len(shards) > 0:
        values = block_scale(rng, shape, shards, -0.22, 0.18) * values
    return jnp.clip(values, min=-bound, max=bound).astype(dtype)


def setup_inputs(seed: int = 0) -> dict:
    arg_keys = jax.random.split(jax.random.key(seed), 5)
    inputs = scatter_about(arg_keys[0], (TOKENS, D), 1.0, 6.0, ((0, 16),))
    cotangent = scatter_about(arg_keys[1], (TOKENS, FF), 0.2, 1.1953125, ((0, 16), (1, 32)))
    gate_weight = scatter_about(arg_keys[2], (D, FF), D ** -0.5, 0.078125, ((0, 16), (1, 32)))
    up_weight = scatter_about(arg_keys[3], (D, FF), D ** -0.5, 0.078125, ((0, 16), (1, 32)))
    return {"inputs": inputs, "cotangent": cotangent, "gate_weight": gate_weight, "up_weight": up_weight}


def reference(inputs, cotangent, gate_weight, up_weight):
    gate_full = jnp.dot(inputs, gate_weight, preferred_element_type=jnp.float32)
    up_full = jnp.dot(inputs, up_weight, preferred_element_type=jnp.float32)
    sigmoid_gate = jax.nn.sigmoid(gate_full)
    cot_wide = cotangent.astype(jnp.float32)
    d_gate = (cot_wide * up_full * sigmoid_gate * (1.0 + gate_full * (1.0 - sigmoid_gate))).astype(jnp.bfloat16)
    d_up = (cot_wide * gate_full * sigmoid_gate).astype(jnp.bfloat16)
    gate_grad = jnp.dot(inputs.T, d_gate, preferred_element_type=jnp.float32).astype(jnp.bfloat16)
    up_grad = jnp.dot(inputs.T, d_up, preferred_element_type=jnp.float32).astype(jnp.bfloat16)
    input_sum = jnp.dot(d_gate, gate_weight.T, preferred_element_type=jnp.float32)
    input_sum = input_sum + jnp.dot(d_up, up_weight.T, preferred_element_type=jnp.float32)
    return input_sum.astype(jnp.bfloat16), gate_grad, up_grad
```

```python
import jax
import jax.numpy as jnp
from jax import lax
from jax.sharding import PartitionSpec as P


def over_tokens(left, right):
    return lax.dot_general(
        left, right, (((0,), (0,)), ((), ())), preferred_element_type=jnp.float32
    )


def over_hidden(left, right):
    return lax.dot_general(
        left, right, (((1,), (1,)), ((), ())), preferred_element_type=jnp.float32
    )


def local_grads(gate_full, up_full, cotangent):
    sigmoid_gate = jax.nn.sigmoid(gate_full)
    cot_wide = cotangent.astype(jnp.float32)
    d_gate = (cot_wide * up_full * sigmoid_gate * (1.0 + gate_full * (1.0 - sigmoid_gate))).astype(
        jnp.bfloat16
    )
    d_up = (cot_wide * gate_full * sigmoid_gate).astype(jnp.bfloat16)
    return (d_gate, d_up)


def shards(rows, cols, inputs, cotangent, gate_weight, up_weight):
    depth, hidden = gate_weight.shape
    own = inputs.shape[0]
    tokens = own * rows
    panels = lax.all_to_all(inputs, "row", split_axis=1, concat_axis=0, tiled=True)
    joined = jnp.concatenate([gate_weight, up_weight], axis=1)
    partial = jnp.dot(panels, joined, preferred_element_type=jnp.float32).astype(jnp.bfloat16)
    parts = lax.all_to_all(partial.reshape(rows, own, 2 * hidden), "row", 0, 0)
    summed = jnp.sum(parts.astype(jnp.float32), axis=0)
    d_gate, d_up = local_grads(summed[:, :hidden], summed[:, hidden:], cotangent)
    d_own = jnp.concatenate([d_gate, d_up], axis=1)
    d_all = lax.all_to_all(jnp.broadcast_to(d_own[None], (rows, own, 2 * hidden)), "row", 0, 0)
    d_all = d_all.reshape(tokens, 2 * hidden)
    input_term = over_hidden(d_all, joined).astype(jnp.bfloat16)
    pieces = lax.all_to_all(input_term.reshape(cols, tokens // cols, depth), "col", 0, 0)
    grads = over_tokens(panels, d_all).astype(jnp.bfloat16)
    input_grad = jnp.sum(pieces.astype(jnp.float32), axis=0).astype(jnp.bfloat16)
    return (input_grad, grads[:, :hidden], grads[:, hidden:])


def solution(mesh):
    in_specs = (P("row", None), P("row", "col"), P("row", "col"), P("row", "col"))
    out_specs = (P("col", "row"), P("row", "col"), P("row", "col"))
    rows, cols = mesh.shape["row"], mesh.shape["col"]

    def local(*arrays):
        return shards(rows, cols, *arrays)

    return jax.shard_map(local, mesh=mesh, in_specs=in_specs, out_specs=out_specs, check_vma=False)
```

```python
import functools

import jax
import jax.numpy as jnp
from jax import lax
from jax.experimental import pallas as pl
from jax.experimental.pallas import tpu as pltpu
from jax.sharding import PartitionSpec as P

GROUP = 8
VMEM_BYTES = 40 * 1024 * 1024

VMEM = pl.BlockSpec(memory_space=pltpu.VMEM)
SMEM = pl.BlockSpec(memory_space=pltpu.SMEM)
BF16, F32 = jnp.bfloat16, jnp.float32


def rows_at(start, size):
    return pl.ds(pl.multiple_of(start * size, size), size)


def lay_kernel(where_ref, tokens_ref, out_ref):
    rows, own, depth = out_ref.shape
    at = rows_at(where_ref[0], own)
    for row in range(rows):
        out_ref[row] = tokens_ref[at, row * depth : (row + 1) * depth]


def forward_kernel(where_ref, mine_ref, other_ref, gate_ref, up_ref, out_ref):
    rows, own, depth = mine_ref.shape
    hidden = gate_ref.shape[1]
    for side_core, tokens_ref in enumerate((mine_ref, other_ref)):
        half = jnp.bitwise_xor(where_ref[0], side_core)
        tokens = tokens_ref[...].reshape(rows * own, depth)
        for i, weight_ref in enumerate((gate_ref, up_ref)):
            total = jnp.dot(tokens, weight_ref[...], preferred_element_type=F32).astype(BF16)
            for row in range(rows):
                side, m = divmod(row, GROUP)
                out_ref[m, rows_at(2 * side + half, own), i * hidden : (i + 1) * hidden] = total[
                    row * own : (row + 1) * own
                ]


def sum_kernel(where_ref, parts_ref, keep_ref, send_ref):
    count = parts_ref.shape[0]
    rows = keep_ref.shape[0]
    for ref, side in ((send_ref, 1 - where_ref[0]), (keep_ref, where_ref[0])):
        at = rows_at(side, rows)
        total = parts_ref[0, at, :].astype(F32)
        for part in range(1, count):
            total += parts_ref[part, at, :].astype(F32)
        ref[...] = total.astype(ref.dtype)


def act_kernel(keep_ref, came_ref, cot_ref, out_ref):
    hidden = cot_ref.shape[1]
    total = keep_ref[...] + came_ref[...].astype(F32)
    gate, up = total[:, :hidden], total[:, hidden:]
    cot = cot_ref[...].astype(F32)
    sig = 1.0 / (1.0 + jnp.exp(-gate))
    out_ref[:, :hidden] = (cot * up * sig * (1.0 + gate * (1.0 - sig))).astype(BF16)
    out_ref[:, hidden:] = (cot * gate * sig).astype(BF16)


def copies_kernel(where_ref, mine_ref, other_ref, out_ref):
    rows = mine_ref.shape[0]
    mine, other = mine_ref[...], other_ref[...]
    for m in range(out_ref.shape[0]):
        out_ref[m, rows_at(where_ref[0], rows), :] = mine
        out_ref[m, rows_at(1 - where_ref[0], rows), :] = other


def half_tokens(d_ref, half, own):
    return jnp.concatenate(
        [
            d_ref[m, rows_at(2 * side + half, own), :]
            for side in range(2)
            for m in range(GROUP)
        ],
        axis=0,
    )


def over_hidden(left, right):
    return lax.dot_general(left, right, (((1,), (1,)), ((), ())), preferred_element_type=F32)


def over_tokens(left, right):
    return lax.dot_general(left, right, (((0,), (0,)), ((), ())), preferred_element_type=F32)


def term_of(half, own, d_ref, gate_ref, up_ref):
    hidden = gate_ref.shape[1]
    d = half_tokens(d_ref, half, own)
    return over_hidden(d[:, :hidden], gate_ref[...]) + over_hidden(d[:, hidden:], up_ref[...])


def other_term_kernel(where_ref, d_ref, gate_ref, up_ref, out_ref):
    own = d_ref.shape[1] // 4
    out_ref[...] = term_of(1 - where_ref[0], own, d_ref, gate_ref, up_ref)


def own_term_kernel(where_ref, d_ref, gate_ref, up_ref, came_ref, out_ref):
    own = d_ref.shape[1] // 4
    total = term_of(where_ref[0], own, d_ref, gate_ref, up_ref) + came_ref[...]
    out_ref[...] = total.astype(BF16).reshape(out_ref.shape)


def weight_grad_kernel(where_ref, mine_ref, other_ref, d_ref, gate_ref, up_ref):
    rows, own, depth = mine_ref.shape
    hidden = gate_ref.shape[1]
    mine = mine_ref[...].reshape(rows * own, depth)
    other = other_ref[...].reshape(rows * own, depth)
    d_mine = half_tokens(d_ref, where_ref[0], own)
    d_other = half_tokens(d_ref, 1 - where_ref[0], own)
    for i, ref in enumerate((gate_ref, up_ref)):
        span = slice(i * hidden, (i + 1) * hidden)
        total = over_tokens(mine, d_mine[:, span]) + over_tokens(other, d_other[:, span])
        ref[...] = total.astype(BF16)


def call(kernel, outs, n_where, n_in, flops=0, nbytes=0):
    return pl.pallas_call(
        kernel,
        out_shape=outs,
        in_specs=[SMEM] * n_where + [VMEM] * n_in,
        out_specs=jax.tree.map(lambda _: VMEM, outs),
        compiler_params=pltpu.CompilerParams(vmem_limit_bytes=VMEM_BYTES),
        cost_estimate=pl.CostEstimate(flops=flops, bytes_accessed=nbytes, transcendentals=0),
    )


def shards(rows, cols, inputs, cotangent, gate_weight, up_weight):
    depth, hidden = gate_weight.shape
    tokens = inputs.shape[0]
    own = tokens // 2
    wide = 2 * hidden
    flops = 2 * rows * tokens * depth * wide
    pairs = [list(range(0, GROUP)), list(range(GROUP, 2 * GROUP))]
    y_groups = [[4 * y + k for y in range(cols // 4)] for k in range(4)]
    row, col = lax.axis_index("row"), lax.axis_index("col")

    def scalar(value):
        return value.astype(jnp.int32).reshape(1)

    side, core = scalar(row // GROUP), scalar(col % 2)
    z_hi = scalar((col // 2) % 2)

    def shape(dims, dtype=BF16):
        return jax.ShapeDtypeStruct(dims, dtype)

    def exchange(array, axis, groups=None):
        return lax.all_to_all(array, axis, 0, 0, axis_index_groups=groups)

    def swap(array, axis, count, bit):
        return lax.ppermute(array, axis, [(i, i ^ bit) for i in range(count)])

    sent = call(lay_kernel, shape((rows, own, depth)), 1, 1)(core, inputs)
    mine = exchange(sent, "row")
    other = swap(mine, "col", cols, 1)

    partial = call(forward_kernel, shape((GROUP, 2 * tokens, wide)), 1, 4, flops)(
        core, mine, other, gate_weight, up_weight
    )
    parts = exchange(partial, "row", pairs)
    keep, send = call(sum_kernel, [shape((tokens, wide), F32), shape((tokens, wide))], 1, 1)(
        side, parts
    )
    came = swap(send, "row", rows, GROUP)
    d_own = call(act_kernel, shape((tokens, wide)), 0, 3)(keep, came, cotangent)
    d_far = swap(d_own, "row", rows, GROUP)
    copies = call(copies_kernel, shape((GROUP, 2 * tokens, wide)), 1, 2)(side, d_own, d_far)
    d_all = exchange(copies, "row", pairs)

    far_term = call(other_term_kernel, shape((rows * own, depth), F32), 1, 3, flops // 2)(
        core, d_all, gate_weight, up_weight
    )
    came_term = swap(far_term, "col", cols, 1)
    term = call(own_term_kernel, shape((rows // 2, 2 * own, depth)), 1, 4, flops // 2)(
        core, d_all, gate_weight, up_weight, came_term
    )
    over_y = exchange(term, "col", y_groups)
    keep, send = call(sum_kernel, [shape((own, depth), F32), shape((own, depth), F32)], 1, 1)(
        z_hi, over_y
    )
    input_grad = (keep + swap(send, "col", cols, 2)).astype(BF16)

    grad = shape((depth, hidden))
    gate_grad, up_grad = call(weight_grad_kernel, [grad, grad], 1, 3, flops)(
        core, mine, other, d_all
    )
    return (input_grad, gate_grad, up_grad)


def solution(mesh):
    in_specs = (P("row", None), P("row", "col"), P("row", "col"), P("row", "col"))
    out_specs = (P("col", "row"), P("row", "col"), P("row", "col"))
    local = functools.partial(shards, mesh.shape["row"], mesh.shape["col"])
    return jax.shard_map(local, mesh=mesh, in_specs=in_specs, out_specs=out_specs, check_vma=False)
```

```python
import functools

import jax
import jax.numpy as jnp
from jax import lax
from jax.experimental import pallas as pl
from jax.experimental.pallas import tpu as pltpu
from jax.sharding import PartitionSpec as P

GROUP = 8
VMEM_BYTES = 40 * 1024 * 1024

VMEM = pl.BlockSpec(memory_space=pltpu.VMEM)
SMEM = pl.BlockSpec(memory_space=pltpu.SMEM)
BF16, F32 = jnp.bfloat16, jnp.float32


def rows_at(start, size):
    return pl.ds(pl.multiple_of(start * size, size), size)


def lay_kernel(half_ref, tokens_ref, out_ref):
    rows, part, depth = out_ref.shape
    at = rows_at(half_ref[0], part)
    for row in range(rows):
        out_ref[row] = tokens_ref[at, row * depth : (row + 1) * depth]


def forward_kernel(tokens_ref, gate_ref, up_ref, out_ref):
    rows, part, depth = tokens_ref.shape
    hidden = gate_ref.shape[1]
    tokens = tokens_ref[...].reshape(rows * part, depth)
    for i, weight_ref in enumerate((gate_ref, up_ref)):
        total = jnp.dot(tokens, weight_ref[...], preferred_element_type=F32).astype(BF16)
        for row in range(rows):
            side, m = divmod(row, GROUP)
            out_ref[m, side * part : (side + 1) * part, i * hidden : (i + 1) * hidden] = total[
                row * part : (row + 1) * part
            ]


def sum_kernel(parts_ref, keep_ref, send_ref):
    total = parts_ref[0].astype(F32)
    for part in range(1, parts_ref.shape[0]):
        total += parts_ref[part].astype(F32)
    keep_ref[...] = total
    send_ref[...] = total.astype(BF16)


def act_kernel(where_ref, keep_ref, came_ref, cot_ref, far_cot_ref, out_ref):
    part = keep_ref.shape[0] // 2
    hidden = cot_ref.shape[1]
    half = rows_at(where_ref[1], part)
    for side, ref in ((where_ref[0], cot_ref), (1 - where_ref[0], far_cot_ref)):
        at = rows_at(side, part)
        cot = ref[half, :].astype(F32)
        total = keep_ref[at, :] + came_ref[at, :].astype(F32)
        gate, up = total[:, :hidden], total[:, hidden:]
        sig = 1.0 / (1.0 + jnp.exp(-gate))
        d_gate = (cot * up * sig * (1.0 + gate * (1.0 - sig))).astype(BF16)
        d_up = (cot * gate * sig).astype(BF16)
        for m in range(out_ref.shape[0]):
            out_ref[m, at, :hidden] = d_gate
            out_ref[m, at, hidden:] = d_up


def by_row(d_ref):
    part = d_ref.shape[1] // 2
    return jnp.concatenate(
        [
            d_ref[m, side * part : (side + 1) * part, :]
            for side in range(2)
            for m in range(GROUP)
        ],
        axis=0,
    )


def over_hidden(left, right):
    return lax.dot_general(left, right, (((1,), (1,)), ((), ())), preferred_element_type=F32)


def over_tokens(left, right):
    return lax.dot_general(left, right, (((0,), (0,)), ((), ())), preferred_element_type=F32)


def term_of(d_ref, gate_ref, up_ref):
    hidden = gate_ref.shape[1]
    d = by_row(d_ref)
    return over_hidden(d[:, :hidden], gate_ref[...]) + over_hidden(d[:, hidden:], up_ref[...])


def far_term_kernel(d_ref, gate_ref, up_ref, out_ref):
    out_ref[...] = term_of(d_ref, gate_ref, up_ref)


def near_term_kernel(d_ref, gate_ref, up_ref, came_ref, out_ref):
    total = term_of(d_ref, gate_ref, up_ref) + came_ref[...]
    out_ref[...] = total.astype(BF16).reshape(out_ref.shape)


def weight_grad_kernel(far_ref, near_ref, d_far_ref, d_near_ref, gate_ref, up_ref):
    rows, part, depth = far_ref.shape
    hidden = gate_ref.shape[1]
    far = far_ref[...].reshape(rows * part, depth)
    near = near_ref[...].reshape(rows * part, depth)
    d_far, d_near = by_row(d_far_ref), by_row(d_near_ref)
    for i, ref in enumerate((gate_ref, up_ref)):
        span = slice(i * hidden, (i + 1) * hidden)
        total = over_tokens(far, d_far[:, span]) + over_tokens(near, d_near[:, span])
        ref[...] = total.astype(BF16)


def call(kernel, outs, n_where, n_in, flops=0, nbytes=0):
    return pl.pallas_call(
        kernel,
        out_shape=outs,
        in_specs=[SMEM] * n_where + [VMEM] * n_in,
        out_specs=jax.tree.map(lambda _: VMEM, outs),
        compiler_params=pltpu.CompilerParams(vmem_limit_bytes=VMEM_BYTES),
        cost_estimate=pl.CostEstimate(flops=flops, bytes_accessed=nbytes, transcendentals=0),
    )


def shards(rows, cols, inputs, cotangent, gate_weight, up_weight):
    depth, hidden = gate_weight.shape
    part = inputs.shape[0] // 2
    wide = 2 * hidden
    flops = 2 * rows * part * depth * wide
    pairs = [list(range(0, GROUP)), list(range(GROUP, 2 * GROUP))]
    core_groups = [[2 * i + core for i in range(cols // 2)] for core in range(2)]
    row, col = lax.axis_index("row"), lax.axis_index("col")

    def scalar(value):
        return value.astype(jnp.int32).reshape(1)

    side = scalar(row // GROUP)
    halves = {"far": scalar(1 - col % 2), "near": scalar(col % 2)}

    def shape(dims, dtype=BF16):
        return jax.ShapeDtypeStruct(dims, dtype)

    def exchange(array, axis, groups=None):
        return lax.all_to_all(array, axis, 0, 0, axis_index_groups=groups)

    def swap(array, axis, count, bit):
        return lax.ppermute(array, axis, [(i, i ^ bit) for i in range(count)])

    sent = call(lay_kernel, shape((rows, part, depth)), 1, 1)(halves["far"], inputs)
    tokens = {"far": exchange(sent, "row")}
    tokens["near"] = swap(tokens["far"], "col", cols, 1)

    far_cot = swap(cotangent, "row", rows, GROUP)
    d = {}
    for half in ("far", "near"):
        partial = call(forward_kernel, shape((GROUP, 2 * part, wide)), 0, 3, flops)(
            tokens[half], gate_weight, up_weight
        )
        parts = exchange(partial, "row", pairs)
        keep, send = call(
            sum_kernel, [shape((2 * part, wide), F32), shape((2 * part, wide))], 0, 1
        )(parts)
        came = swap(send, "row", rows, GROUP)
        copies = call(act_kernel, shape((GROUP, 2 * part, wide)), 1, 4)(
            jnp.concatenate([side, halves[half]]), keep, came, cotangent, far_cot
        )
        d[half] = exchange(copies, "row", pairs)

    far_term = call(far_term_kernel, shape((rows * part, depth), F32), 0, 3, flops)(
        d["far"], gate_weight, up_weight
    )
    came = swap(far_term, "col", cols, 1)
    term = call(near_term_kernel, shape((rows, part, depth)), 0, 4, flops)(
        d["near"], gate_weight, up_weight, came
    )
    over_col = exchange(term, "col", core_groups)
    input_grad = jnp.sum(over_col.astype(F32), axis=0).astype(BF16)

    grad = shape((depth, hidden))
    gate_grad, up_grad = call(weight_grad_kernel, [grad, grad], 0, 4, 2 * flops)(
        tokens["far"], tokens["near"], d["far"], d["near"]
    )
    return (input_grad, gate_grad, up_grad)


def solution(mesh):
    in_specs = (P("row", None), P("row", "col"), P("row", "col"), P("row", "col"))
    out_specs = (P("col", "row"), P("row", "col"), P("row", "col"))
    local = functools.partial(shards, mesh.shape["row"], mesh.shape["col"])
    return jax.shard_map(local, mesh=mesh, in_specs=in_specs, out_specs=out_specs, check_vma=False)
```

```python
import functools

import jax
import jax.numpy as jnp
from jax import lax
from jax.experimental import pallas as pl
from jax.experimental.pallas import tpu as pltpu
from jax.sharding import PartitionSpec as P

GROUP = 8
VMEM_BYTES = 40 * 1024 * 1024

VMEM = pl.BlockSpec(memory_space=pltpu.VMEM)
SMEM = pl.BlockSpec(memory_space=pltpu.SMEM)
ANY = pl.BlockSpec(memory_space=pl.ANY)
BF16, F32 = jnp.bfloat16, jnp.float32


def rows_at(start, size):
    return pl.ds(pl.multiple_of(start * size, size), size)


def lay_kernel(half_ref, tokens_ref, out_ref):
    rows, part, depth = out_ref.shape
    at = rows_at(half_ref[0], part)
    for row in range(rows):
        out_ref[row] = tokens_ref[at, row * depth : (row + 1) * depth]


def stage_kernel(gate_ref, up_ref, gate_out_ref, up_out_ref):
    gate_out_ref[...] = gate_ref[...]
    up_out_ref[...] = up_ref[...]


def forward_kernel(tokens_ref, gate_ref, up_ref, _, out_ref):
    rows, part, depth = tokens_ref.shape
    hidden = gate_ref.shape[1]
    tokens = tokens_ref[...].reshape(rows * part, depth)
    for i, weight_ref in enumerate((gate_ref, up_ref)):
        total = jnp.dot(tokens, weight_ref[...], preferred_element_type=F32).astype(BF16)
        for row in range(rows):
            side, m = divmod(row, GROUP)
            out_ref[m, side * part : (side + 1) * part, i * hidden : (i + 1) * hidden] = total[
                row * part : (row + 1) * part
            ]


def sum_kernel(parts_ref, keep_ref, send_ref):
    total = parts_ref[0].astype(F32)
    for part in range(1, parts_ref.shape[0]):
        total += parts_ref[part].astype(F32)
    keep_ref[...] = total
    send_ref[...] = total.astype(BF16)


def act_kernel(where_ref, keep_ref, came_ref, cot_ref, far_cot_ref, out_ref):
    part = keep_ref.shape[0] // 2
    hidden = cot_ref.shape[1]
    half = rows_at(where_ref[1], part)
    for side, ref in ((where_ref[0], cot_ref), (1 - where_ref[0], far_cot_ref)):
        at = rows_at(side, part)
        cot = ref[half, :].astype(F32)
        total = keep_ref[at, :] + came_ref[at, :].astype(F32)
        gate, up = total[:, :hidden], total[:, hidden:]
        sig = 1.0 / (1.0 + jnp.exp(-gate))
        d_gate = (cot * up * sig * (1.0 + gate * (1.0 - sig))).astype(BF16)
        d_up = (cot * gate * sig).astype(BF16)
        for m in range(out_ref.shape[0]):
            out_ref[m, at, :hidden] = d_gate
            out_ref[m, at, hidden:] = d_up


def by_row(d_ref):
    part = d_ref.shape[1] // 2
    return jnp.concatenate(
        [
            d_ref[m, side * part : (side + 1) * part, :]
            for side in range(2)
            for m in range(GROUP)
        ],
        axis=0,
    )


def over_hidden(left, right):
    return lax.dot_general(left, right, (((1,), (1,)), ((), ())), preferred_element_type=F32)


def over_tokens(left, right):
    return lax.dot_general(left, right, (((0,), (0,)), ((), ())), preferred_element_type=F32)


def term_of(d_ref, gate_ref, up_ref):
    hidden = gate_ref.shape[1]
    d = by_row(d_ref)
    return over_hidden(d[:, :hidden], gate_ref[...]) + over_hidden(d[:, hidden:], up_ref[...])


def far_term_kernel(d_ref, gate_ref, up_ref, out_ref):
    out_ref[...] = term_of(d_ref, gate_ref, up_ref)


def near_term_kernel(d_ref, gate_ref, up_ref, came_ref, out_ref):
    total = term_of(d_ref, gate_ref, up_ref) + came_ref[...]
    out_ref[...] = total.astype(BF16).reshape(out_ref.shape)


def weight_grad_kernel(far_ref, near_ref, d_far_ref, d_near_ref, gate_ref, up_ref):
    rows, part, depth = far_ref.shape
    hidden = gate_ref.shape[1]
    far = far_ref[...].reshape(rows * part, depth)
    near = near_ref[...].reshape(rows * part, depth)
    d_far, d_near = by_row(d_far_ref), by_row(d_near_ref)
    for i, ref in enumerate((gate_ref, up_ref)):
        span = slice(i * hidden, (i + 1) * hidden)
        total = over_tokens(far, d_far[:, span]) + over_tokens(near, d_near[:, span])
        ref[...] = total.astype(BF16)


def call(kernel, outs, n_where, n_in, flops=0, nbytes=0, n_any=0):
    return pl.pallas_call(
        kernel,
        out_shape=outs,
        in_specs=[SMEM] * n_where + [VMEM] * n_in + [ANY] * n_any,
        out_specs=jax.tree.map(lambda _: VMEM, outs),
        compiler_params=pltpu.CompilerParams(vmem_limit_bytes=VMEM_BYTES),
        cost_estimate=pl.CostEstimate(flops=flops, bytes_accessed=nbytes, transcendentals=0),
    )


def shards(rows, cols, inputs, cotangent, gate_weight, up_weight):
    depth, hidden = gate_weight.shape
    part = inputs.shape[0] // 2
    wide = 2 * hidden
    flops = 2 * rows * part * depth * wide
    pairs = [list(range(0, GROUP)), list(range(GROUP, 2 * GROUP))]
    core_groups = [[2 * i + core for i in range(cols // 2)] for core in range(2)]
    row, col = lax.axis_index("row"), lax.axis_index("col")

    def scalar(value):
        return value.astype(jnp.int32).reshape(1)

    side = scalar(row // GROUP)
    halves = {"far": scalar(1 - col % 2), "near": scalar(col % 2)}

    def shape(dims, dtype=BF16):
        return jax.ShapeDtypeStruct(dims, dtype)

    def exchange(array, axis, groups=None):
        return lax.all_to_all(array, axis, 0, 0, axis_index_groups=groups)

    def swap(array, axis, count, bit):
        return lax.ppermute(array, axis, [(i, i ^ bit) for i in range(count)])

    sent = call(lay_kernel, shape((rows, part, depth)), 1, 1)(halves["far"], inputs)
    tokens = {"far": exchange(sent, "row")}
    tokens["near"] = swap(tokens["far"], "col", cols, 1)

    grad = shape((depth, hidden))
    gate, up = call(stage_kernel, [grad, grad], 0, 2, nbytes=8 * depth * hidden)(
        gate_weight, up_weight
    )
    far_cot = swap(cotangent, "row", rows, GROUP)
    d = {}
    for half in ("far", "near"):
        partial = call(forward_kernel, shape((GROUP, 2 * part, wide)), 0, 3, flops, n_any=1)(
            tokens[half], gate, up, far_cot if half == "near" else side
        )
        parts = exchange(partial, "row", pairs)
        keep, send = call(
            sum_kernel, [shape((2 * part, wide), F32), shape((2 * part, wide))], 0, 1
        )(parts)
        came = swap(send, "row", rows, GROUP)
        copies = call(act_kernel, shape((GROUP, 2 * part, wide)), 1, 4)(
            jnp.concatenate([side, halves[half]]), keep, came, cotangent, far_cot
        )
        d[half] = exchange(copies, "row", pairs)

    far_term = call(far_term_kernel, shape((rows * part, depth), F32), 0, 3, flops)(
        d["far"], gate, up
    )
    came = swap(far_term, "col", cols, 1)
    term = call(near_term_kernel, shape((rows, part, depth)), 0, 4, flops)(
        d["near"], gate, up, came
    )
    over_col = exchange(term, "col", core_groups)
    input_grad = jnp.sum(over_col.astype(F32), axis=0).astype(BF16)

    gate_grad, up_grad = call(weight_grad_kernel, [grad, grad], 0, 4, 2 * flops)(
        tokens["far"], tokens["near"], d["far"], d["near"]
    )
    return (input_grad, gate_grad, up_grad)


def solution(mesh):
    in_specs = (P("row", None), P("row", "col"), P("row", "col"), P("row", "col"))
    out_specs = (P("col", "row"), P("row", "col"), P("row", "col"))
    local = functools.partial(shards, mesh.shape["row"], mesh.shape["col"])
    return jax.shard_map(local, mesh=mesh, in_specs=in_specs, out_specs=out_specs, check_vma=False)
```

```python
import functools

import jax
import jax.numpy as jnp
from jax import lax
from jax.experimental import pallas as pl
from jax.experimental.pallas import tpu as pltpu
from jax.sharding import PartitionSpec as P

GROUP = 8
VMEM_BYTES = 40 * 1024 * 1024

VMEM = pl.BlockSpec(memory_space=pltpu.VMEM)
SMEM = pl.BlockSpec(memory_space=pltpu.SMEM)
ANY = pl.BlockSpec(memory_space=pl.ANY)
BF16, F32 = jnp.bfloat16, jnp.float32


def rows_at(start, size):
    return pl.ds(pl.multiple_of(start * size, size), size)


def stage_kernel(gate_ref, up_ref, gate_out_ref, up_out_ref):
    gate_out_ref[...] = gate_ref[...]
    up_out_ref[...] = up_ref[...]


def forward_kernel(tokens_ref, gate_ref, up_ref, _, out_ref):
    rows, part, depth = tokens_ref.shape
    hidden = gate_ref.shape[1]
    tokens = tokens_ref[...].reshape(rows * part, depth)
    for i, weight_ref in enumerate((gate_ref, up_ref)):
        total = jnp.dot(tokens, weight_ref[...], preferred_element_type=F32).astype(BF16)
        for row in range(rows):
            side, m = divmod(row, GROUP)
            out_ref[m, side * part : (side + 1) * part, i * hidden : (i + 1) * hidden] = total[
                row * part : (row + 1) * part
            ]


def sum_kernel(parts_ref, keep_ref, send_ref):
    total = parts_ref[0].astype(F32)
    for part in range(1, parts_ref.shape[0]):
        total += parts_ref[part].astype(F32)
    keep_ref[...] = total
    send_ref[...] = total.astype(BF16)


def act_kernel(where_ref, keep_ref, came_ref, cot_ref, far_cot_ref, out_ref):
    part = keep_ref.shape[0] // 2
    hidden = cot_ref.shape[1]
    half = rows_at(where_ref[1], part)
    for side, ref in ((where_ref[0], cot_ref), (1 - where_ref[0], far_cot_ref)):
        at = rows_at(side, part)
        cot = ref[half, :].astype(F32)
        total = keep_ref[at, :] + came_ref[at, :].astype(F32)
        gate, up = total[:, :hidden], total[:, hidden:]
        sig = 1.0 / (1.0 + jnp.exp(-gate))
        d_gate = (cot * up * sig * (1.0 + gate * (1.0 - sig))).astype(BF16)
        d_up = (cot * gate * sig).astype(BF16)
        for m in range(out_ref.shape[0]):
            out_ref[m, at, :hidden] = d_gate
            out_ref[m, at, hidden:] = d_up


def by_row(d_ref):
    part = d_ref.shape[1] // 2
    return jnp.concatenate(
        [
            d_ref[m, side * part : (side + 1) * part, :]
            for side in range(2)
            for m in range(GROUP)
        ],
        axis=0,
    )


def over_hidden(left, right):
    return lax.dot_general(left, right, (((1,), (1,)), ((), ())), preferred_element_type=F32)


def over_tokens(left, right):
    return lax.dot_general(left, right, (((0,), (0,)), ((), ())), preferred_element_type=F32)


def term_of(d_ref, gate_ref, up_ref):
    hidden = gate_ref.shape[1]
    d = by_row(d_ref)
    return over_hidden(d[:, :hidden], gate_ref[...]) + over_hidden(d[:, hidden:], up_ref[...])


def far_term_kernel(d_ref, gate_ref, up_ref, out_ref):
    out_ref[...] = term_of(d_ref, gate_ref, up_ref).astype(BF16)


def near_term_kernel(d_ref, gate_ref, up_ref, came_ref, out_ref):
    total = term_of(d_ref, gate_ref, up_ref) + came_ref[...].astype(F32)
    out_ref[...] = total.astype(BF16).reshape(out_ref.shape)


def weight_grad_kernel(far_ref, near_ref, d_far_ref, d_near_ref, gate_ref, up_ref):
    rows, part, depth = far_ref.shape
    hidden = gate_ref.shape[1]
    far = far_ref[...].reshape(rows * part, depth)
    near = near_ref[...].reshape(rows * part, depth)
    d_far, d_near = by_row(d_far_ref), by_row(d_near_ref)
    for i, ref in enumerate((gate_ref, up_ref)):
        span = slice(i * hidden, (i + 1) * hidden)
        total = over_tokens(far, d_far[:, span]) + over_tokens(near, d_near[:, span])
        ref[...] = total.astype(BF16)


def call(kernel, outs, n_where, n_in, flops=0, nbytes=0, n_any=0):
    return pl.pallas_call(
        kernel,
        out_shape=outs,
        in_specs=[SMEM] * n_where + [VMEM] * n_in + [ANY] * n_any,
        out_specs=jax.tree.map(lambda _: VMEM, outs),
        compiler_params=pltpu.CompilerParams(vmem_limit_bytes=VMEM_BYTES),
        cost_estimate=pl.CostEstimate(flops=flops, bytes_accessed=nbytes, transcendentals=0),
    )


def shards(rows, cols, inputs, cotangent, gate_weight, up_weight):
    depth, hidden = gate_weight.shape
    part = inputs.shape[0] // 2
    wide = 2 * hidden
    flops = 2 * rows * part * depth * wide
    pairs = [list(range(0, GROUP)), list(range(GROUP, 2 * GROUP))]
    core_groups = [[2 * i + core for i in range(cols // 2)] for core in range(2)]
    row, col = lax.axis_index("row"), lax.axis_index("col")

    def scalar(value):
        return value.astype(jnp.int32).reshape(1)

    side = scalar(row // GROUP)
    halves = {"far": scalar(1 - col % 2), "near": scalar(col % 2)}

    def shape(dims, dtype=BF16):
        return jax.ShapeDtypeStruct(dims, dtype)

    def exchange(array, axis, groups=None):
        return lax.all_to_all(array, axis, 0, 0, axis_index_groups=groups)

    def swap(array, axis, count, bit):
        return lax.ppermute(array, axis, [(i, i ^ bit) for i in range(count)])

    sent = lax.dynamic_slice_in_dim(inputs, halves["far"][0] * part, part, axis=0)
    sent = sent.reshape(part, rows, depth).transpose(1, 0, 2)
    tokens = {"far": exchange(sent, "row")}
    tokens["near"] = swap(tokens["far"], "col", cols, 1)

    grad = shape((depth, hidden))
    gate, up = gate_weight, up_weight
    far_cot = swap(cotangent, "row", rows, GROUP)
    d = {}
    for half in ("far", "near"):
        partial = call(forward_kernel, shape((GROUP, 2 * part, wide)), 0, 3, flops, n_any=1)(
            tokens[half], gate, up, far_cot if half == "near" else side
        )
        parts = exchange(partial, "row", pairs)
        keep, send = call(
            sum_kernel, [shape((2 * part, wide), F32), shape((2 * part, wide))], 0, 1
        )(parts)
        came = swap(send, "row", rows, GROUP)
        copies = call(act_kernel, shape((GROUP, 2 * part, wide)), 1, 4)(
            jnp.concatenate([side, halves[half]]), keep, came, cotangent, far_cot
        )
        d[half] = exchange(copies, "row", pairs)

    far_term = call(far_term_kernel, shape((rows * part, depth)), 0, 3, flops)(
        d["far"], gate, up
    )
    came = swap(far_term, "col", cols, 1)
    term = call(near_term_kernel, shape((rows, part, depth)), 0, 4, flops)(
        d["near"], gate, up, came
    )
    over_col = exchange(term, "col", core_groups)
    input_grad = jnp.sum(over_col.astype(F32), axis=0).astype(BF16)

    gate_grad, up_grad = call(weight_grad_kernel, [grad, grad], 0, 4, 2 * flops)(
        tokens["far"], tokens["near"], d["far"], d["near"]
    )
    return (input_grad, gate_grad, up_grad)


def solution(mesh):
    in_specs = (P("row", None), P("row", "col"), P("row", "col"), P("row", "col"))
    out_specs = (P("col", "row"), P("row", "col"), P("row", "col"))
    local = functools.partial(shards, mesh.shape["row"], mesh.shape["col"])
    return jax.shard_map(local, mesh=mesh, in_specs=in_specs, out_specs=out_specs, check_vma=False)
```

```python
import functools

import jax
import jax.numpy as jnp
from jax import lax
from jax.experimental import pallas as pl
from jax.experimental.pallas import tpu as pltpu
from jax.sharding import PartitionSpec as P

GROUP = 8
VMEM_BYTES = 40 * 1024 * 1024

VMEM = pl.BlockSpec(memory_space=pltpu.VMEM)
SMEM = pl.BlockSpec(memory_space=pltpu.SMEM)
ANY = pl.BlockSpec(memory_space=pl.ANY)
BF16, F32 = jnp.bfloat16, jnp.float32


def rows_at(start, size):
    return pl.ds(pl.multiple_of(start * size, size), size)


def lay_kernel(half_ref, tokens_ref, out_ref):
    rows, part, depth = out_ref.shape
    at = rows_at(half_ref[0], part)
    for row in range(rows):
        out_ref[row] = tokens_ref[at, row * depth : (row + 1) * depth]


def stage_kernel(gate_ref, up_ref, gate_out_ref, up_out_ref):
    gate_out_ref[...] = gate_ref[...]
    up_out_ref[...] = up_ref[...]


def forward_kernel(tokens_ref, gate_ref, up_ref, _, out_ref):
    rows, part, depth = tokens_ref.shape
    hidden = gate_ref.shape[1]
    tokens = tokens_ref[...].reshape(rows * part, depth)
    for i, weight_ref in enumerate((gate_ref, up_ref)):
        total = jnp.dot(tokens, weight_ref[...], preferred_element_type=F32).astype(BF16)
        for row in range(rows):
            side, m = divmod(row, GROUP)
            out_ref[m, side * part : (side + 1) * part, i * hidden : (i + 1) * hidden] = total[
                row * part : (row + 1) * part
            ]


def sum_kernel(parts_ref, keep_ref, send_ref):
    total = parts_ref[0].astype(F32)
    for part in range(1, parts_ref.shape[0]):
        total += parts_ref[part].astype(F32)
    keep_ref[...] = total
    send_ref[...] = total.astype(BF16)


def act_kernel(where_ref, keep_ref, came_ref, cot_ref, far_cot_ref, out_ref):
    part = keep_ref.shape[0] // 2
    hidden = cot_ref.shape[1]
    half = rows_at(where_ref[1], part)
    for side, ref in ((where_ref[0], cot_ref), (1 - where_ref[0], far_cot_ref)):
        at = rows_at(side, part)
        cot = ref[half, :].astype(F32)
        total = keep_ref[at, :] + came_ref[at, :].astype(F32)
        gate, up = total[:, :hidden], total[:, hidden:]
        sig = 1.0 / (1.0 + jnp.exp(-gate))
        d_gate = (cot * up * sig * (1.0 + gate * (1.0 - sig))).astype(BF16)
        d_up = (cot * gate * sig).astype(BF16)
        for m in range(out_ref.shape[0]):
            out_ref[m, at, :hidden] = d_gate
            out_ref[m, at, hidden:] = d_up


def by_row(d_ref):
    part = d_ref.shape[1] // 2
    return jnp.concatenate(
        [
            d_ref[m, side * part : (side + 1) * part, :]
            for side in range(2)
            for m in range(GROUP)
        ],
        axis=0,
    )


def over_hidden(left, right):
    return lax.dot_general(left, right, (((1,), (1,)), ((), ())), preferred_element_type=F32)


def over_tokens(left, right):
    return lax.dot_general(left, right, (((0,), (0,)), ((), ())), preferred_element_type=F32)


def term_of(d_ref, gate_ref, up_ref):
    hidden = gate_ref.shape[1]
    d = by_row(d_ref)
    return over_hidden(d[:, :hidden], gate_ref[...]) + over_hidden(d[:, hidden:], up_ref[...])


def far_term_kernel(d_ref, gate_ref, up_ref, out_ref):
    out_ref[...] = term_of(d_ref, gate_ref, up_ref)


def by_z_hi(rows):
    return [2 * y + z_hi for z_hi in range(2) for y in range(rows // 2)]


def near_term_kernel(d_ref, gate_ref, up_ref, came_ref, out_ref):
    rows, part, _ = out_ref.shape
    total = (term_of(d_ref, gate_ref, up_ref) + came_ref[...]).astype(BF16)
    for i, row in enumerate(by_z_hi(rows)):
        out_ref[i] = total[row * part : (row + 1) * part]


def weight_grad_kernel(far_ref, near_ref, d_far_ref, d_near_ref, gate_ref, up_ref):
    rows, part, depth = far_ref.shape
    hidden = gate_ref.shape[1]
    far = far_ref[...].reshape(rows * part, depth)
    near = near_ref[...].reshape(rows * part, depth)
    d_far, d_near = by_row(d_far_ref), by_row(d_near_ref)
    for i, ref in enumerate((gate_ref, up_ref)):
        span = slice(i * hidden, (i + 1) * hidden)
        total = over_tokens(far, d_far[:, span]) + over_tokens(near, d_near[:, span])
        ref[...] = total.astype(BF16)


def call(kernel, outs, n_where, n_in, flops=0, nbytes=0, n_any=0):
    return pl.pallas_call(
        kernel,
        out_shape=outs,
        in_specs=[SMEM] * n_where + [VMEM] * n_in + [ANY] * n_any,
        out_specs=jax.tree.map(lambda _: VMEM, outs),
        compiler_params=pltpu.CompilerParams(vmem_limit_bytes=VMEM_BYTES),
        cost_estimate=pl.CostEstimate(flops=flops, bytes_accessed=nbytes, transcendentals=0),
    )


def shards(rows, cols, inputs, cotangent, gate_weight, up_weight):
    depth, hidden = gate_weight.shape
    part = inputs.shape[0] // 2
    wide = 2 * hidden
    flops = 2 * rows * part * depth * wide
    pairs = [list(range(0, GROUP)), list(range(GROUP, 2 * GROUP))]
    core_groups = [[2 * r + core for r in by_z_hi(rows)] for core in range(2)]
    row, col = lax.axis_index("row"), lax.axis_index("col")

    def scalar(value):
        return value.astype(jnp.int32).reshape(1)

    side = scalar(row // GROUP)
    halves = {"far": scalar(1 - col % 2), "near": scalar(col % 2)}

    def shape(dims, dtype=BF16):
        return jax.ShapeDtypeStruct(dims, dtype)

    def exchange(array, axis, groups=None):
        return lax.all_to_all(array, axis, 0, 0, axis_index_groups=groups)

    def swap(array, axis, count, bit):
        return lax.ppermute(array, axis, [(i, i ^ bit) for i in range(count)])

    sent = call(lay_kernel, shape((rows, part, depth)), 1, 1)(halves["far"], inputs)
    tokens = {"far": exchange(sent, "row")}
    tokens["near"] = swap(tokens["far"], "col", cols, 1)

    grad = shape((depth, hidden))
    gate, up = call(stage_kernel, [grad, grad], 0, 2, nbytes=8 * depth * hidden)(
        gate_weight, up_weight
    )
    far_cot = swap(cotangent, "row", rows, GROUP)
    d = {}
    for half in ("far", "near"):
        partial = call(forward_kernel, shape((GROUP, 2 * part, wide)), 0, 3, flops, n_any=1)(
            tokens[half], gate, up, far_cot if half == "near" else side
        )
        parts = exchange(partial, "row", pairs)
        keep, send = call(
            sum_kernel, [shape((2 * part, wide), F32), shape((2 * part, wide))], 0, 1
        )(parts)
        came = swap(send, "row", rows, GROUP)
        copies = call(act_kernel, shape((GROUP, 2 * part, wide)), 1, 4)(
            jnp.concatenate([side, halves[half]]), keep, came, cotangent, far_cot
        )
        d[half] = exchange(copies, "row", pairs)

    far_term = call(far_term_kernel, shape((rows * part, depth), F32), 0, 3, flops)(
        d["far"], gate, up
    )
    came = swap(far_term, "col", cols, 1)
    term = call(near_term_kernel, shape((rows, part, depth)), 0, 4, flops)(
        d["near"], gate, up, came
    )
    over_col = exchange(term, "col", core_groups)
    input_grad = jnp.sum(over_col.astype(F32), axis=0).astype(BF16)

    gate_grad, up_grad = call(weight_grad_kernel, [grad, grad], 0, 4, 2 * flops)(
        tokens["far"], tokens["near"], d["far"], d["near"]
    )
    return (input_grad, gate_grad, up_grad)


def solution(mesh):
    in_specs = (P("row", None), P("row", "col"), P("row", "col"), P("row", "col"))
    out_specs = (P("col", "row"), P("row", "col"), P("row", "col"))
    local = functools.partial(shards, mesh.shape["row"], mesh.shape["col"])
    return jax.shard_map(local, mesh=mesh, in_specs=in_specs, out_specs=out_specs, check_vma=False)
```

```python
import functools

import jax
import jax.numpy as jnp
from jax import lax
from jax.experimental import pallas as pl
from jax.experimental.pallas import tpu as pltpu
from jax.sharding import PartitionSpec as P

GROUP = 8
ORDER = (0, 4, 1, 5, 2, 6, 3, 7)
VMEM_BYTES = 40 * 1024 * 1024

VMEM = pl.BlockSpec(memory_space=pltpu.VMEM)
SMEM = pl.BlockSpec(memory_space=pltpu.SMEM)
ANY = pl.BlockSpec(memory_space=pl.ANY)
BF16, F32 = jnp.bfloat16, jnp.float32


def rows_at(start, size):
    return pl.ds(pl.multiple_of(start * size, size), size)


def lay_kernel(half_ref, tokens_ref, out_ref):
    rows, part, depth = out_ref.shape
    at = rows_at(half_ref[0], part)
    for row in range(rows):
        out_ref[row] = tokens_ref[at, row * depth : (row + 1) * depth]


def stage_kernel(gate_ref, up_ref, gate_out_ref, up_out_ref):
    gate_out_ref[...] = gate_ref[...]
    up_out_ref[...] = up_ref[...]


def forward_kernel(tokens_ref, gate_ref, up_ref, _, out_ref):
    rows, part, depth = tokens_ref.shape
    hidden = gate_ref.shape[1]
    tokens = tokens_ref[...].reshape(rows * part, depth)
    for i, weight_ref in enumerate((gate_ref, up_ref)):
        total = jnp.dot(tokens, weight_ref[...], preferred_element_type=F32).astype(BF16)
        for row in range(rows):
            side, m = divmod(row, GROUP)
            out_ref[ORDER.index(m), side * part : (side + 1) * part, i * hidden : (i + 1) * hidden] = total[
                row * part : (row + 1) * part
            ]


def sum_kernel(parts_ref, keep_ref, send_ref):
    total = parts_ref[0].astype(F32)
    for part in range(1, parts_ref.shape[0]):
        total += parts_ref[part].astype(F32)
    keep_ref[...] = total
    send_ref[...] = total.astype(BF16)


def act_kernel(where_ref, keep_ref, came_ref, cot_ref, far_cot_ref, out_ref):
    part = keep_ref.shape[0] // 2
    hidden = cot_ref.shape[1]
    half = rows_at(where_ref[1], part)
    for side, ref in ((where_ref[0], cot_ref), (1 - where_ref[0], far_cot_ref)):
        at = rows_at(side, part)
        cot = ref[half, :].astype(F32)
        total = keep_ref[at, :] + came_ref[at, :].astype(F32)
        gate, up = total[:, :hidden], total[:, hidden:]
        sig = 1.0 / (1.0 + jnp.exp(-gate))
        d_gate = (cot * up * sig * (1.0 + gate * (1.0 - sig))).astype(BF16)
        d_up = (cot * gate * sig).astype(BF16)
        for m in range(out_ref.shape[0]):
            out_ref[m, at, :hidden] = d_gate
            out_ref[m, at, hidden:] = d_up


def by_row(d_ref):
    part = d_ref.shape[1] // 2
    return jnp.concatenate(
        [
            d_ref[ORDER.index(m), side * part : (side + 1) * part, :]
            for side in range(2)
            for m in range(GROUP)
        ],
        axis=0,
    )


def over_hidden(left, right):
    return lax.dot_general(left, right, (((1,), (1,)), ((), ())), preferred_element_type=F32)


def over_tokens(left, right):
    return lax.dot_general(left, right, (((0,), (0,)), ((), ())), preferred_element_type=F32)


def term_of(d_ref, gate_ref, up_ref):
    hidden = gate_ref.shape[1]
    d = by_row(d_ref)
    return over_hidden(d[:, :hidden], gate_ref[...]) + over_hidden(d[:, hidden:], up_ref[...])


def far_term_kernel(d_ref, gate_ref, up_ref, out_ref):
    out_ref[...] = term_of(d_ref, gate_ref, up_ref)


def by_z_hi(rows):
    return [2 * y + z_hi for z_hi in range(2) for y in range(rows // 2)]


def near_term_kernel(d_ref, gate_ref, up_ref, came_ref, out_ref):
    rows, part, _ = out_ref.shape
    total = (term_of(d_ref, gate_ref, up_ref) + came_ref[...]).astype(BF16)
    for i, row in enumerate(by_z_hi(rows)):
        out_ref[i] = total[row * part : (row + 1) * part]


def weight_grad_kernel(far_ref, near_ref, d_far_ref, d_near_ref, gate_ref, up_ref):
    rows, part, depth = far_ref.shape
    hidden = gate_ref.shape[1]
    far = far_ref[...].reshape(rows * part, depth)
    near = near_ref[...].reshape(rows * part, depth)
    d_far, d_near = by_row(d_far_ref), by_row(d_near_ref)
    for i, ref in enumerate((gate_ref, up_ref)):
        span = slice(i * hidden, (i + 1) * hidden)
        total = over_tokens(far, d_far[:, span]) + over_tokens(near, d_near[:, span])
        ref[...] = total.astype(BF16)


def call(kernel, outs, n_where, n_in, flops=0, nbytes=0, n_any=0):
    return pl.pallas_call(
        kernel,
        out_shape=outs,
        in_specs=[SMEM] * n_where + [VMEM] * n_in + [ANY] * n_any,
        out_specs=jax.tree.map(lambda _: VMEM, outs),
        compiler_params=pltpu.CompilerParams(vmem_limit_bytes=VMEM_BYTES),
        cost_estimate=pl.CostEstimate(flops=flops, bytes_accessed=nbytes, transcendentals=0),
    )


def shards(rows, cols, inputs, cotangent, gate_weight, up_weight):
    depth, hidden = gate_weight.shape
    part = inputs.shape[0] // 2
    wide = 2 * hidden
    flops = 2 * rows * part * depth * wide
    pairs = [[start + m for m in ORDER] for start in (0, GROUP)]
    core_groups = [[2 * r + core for r in by_z_hi(rows)] for core in range(2)]
    row, col = lax.axis_index("row"), lax.axis_index("col")

    def scalar(value):
        return value.astype(jnp.int32).reshape(1)

    side = scalar(row // GROUP)
    halves = {"far": scalar(1 - col % 2), "near": scalar(col % 2)}

    def shape(dims, dtype=BF16):
        return jax.ShapeDtypeStruct(dims, dtype)

    def exchange(array, axis, groups=None):
        return lax.all_to_all(array, axis, 0, 0, axis_index_groups=groups)

    def swap(array, axis, count, bit):
        return lax.ppermute(array, axis, [(i, i ^ bit) for i in range(count)])

    sent = call(lay_kernel, shape((rows, part, depth)), 1, 1)(halves["far"], inputs)
    tokens = {"far": exchange(sent, "row")}
    tokens["near"] = swap(tokens["far"], "col", cols, 1)

    grad = shape((depth, hidden))
    gate, up = call(stage_kernel, [grad, grad], 0, 2, nbytes=8 * depth * hidden)(
        gate_weight, up_weight
    )
    far_cot = swap(cotangent, "row", rows, GROUP)
    d = {}
    for half in ("far", "near"):
        partial = call(forward_kernel, shape((GROUP, 2 * part, wide)), 0, 3, flops, n_any=1)(
            tokens[half], gate, up, far_cot if half == "near" else side
        )
        parts = exchange(partial, "row", pairs)
        keep, send = call(
            sum_kernel, [shape((2 * part, wide), F32), shape((2 * part, wide))], 0, 1
        )(parts)
        came = swap(send, "row", rows, GROUP)
        copies = call(act_kernel, shape((GROUP, 2 * part, wide)), 1, 4)(
            jnp.concatenate([side, halves[half]]), keep, came, cotangent, far_cot
        )
        d[half] = exchange(copies, "row", pairs)

    far_term = call(far_term_kernel, shape((rows * part, depth), F32), 0, 3, flops)(
        d["far"], gate, up
    )
    came = swap(far_term, "col", cols, 1)
    term = call(near_term_kernel, shape((rows, part, depth)), 0, 4, flops)(
        d["near"], gate, up, came
    )
    over_col = exchange(term, "col", core_groups)
    input_grad = jnp.sum(over_col.astype(F32), axis=0).astype(BF16)

    gate_grad, up_grad = call(weight_grad_kernel, [grad, grad], 0, 4, 2 * flops)(
        tokens["far"], tokens["near"], d["far"], d["near"]
    )
    return (input_grad, gate_grad, up_grad)


def solution(mesh):
    in_specs = (P("row", None), P("row", "col"), P("row", "col"), P("row", "col"))
    out_specs = (P("col", "row"), P("row", "col"), P("row", "col"))
    local = functools.partial(shards, mesh.shape["row"], mesh.shape["col"])
    return jax.shard_map(local, mesh=mesh, in_specs=in_specs, out_specs=out_specs, check_vma=False)
```

```python
import functools

import jax
import jax.numpy as jnp
from jax import lax
from jax.experimental import pallas as pl
from jax.experimental.pallas import tpu as pltpu
from jax.sharding import PartitionSpec as P

GROUP = 8
VMEM_BYTES = 40 * 1024 * 1024

VMEM = pl.BlockSpec(memory_space=pltpu.VMEM)
SMEM = pl.BlockSpec(memory_space=pltpu.SMEM)
ANY = pl.BlockSpec(memory_space=pl.ANY)
BF16, F32 = jnp.bfloat16, jnp.float32


def rows_at(start, size):
    return pl.ds(pl.multiple_of(start * size, size), size)


def lay_kernel(half_ref, tokens_ref, out_ref):
    rows, part, depth = out_ref.shape
    at = rows_at(half_ref[0], part)
    for row in range(rows):
        out_ref[row] = tokens_ref[at, row * depth : (row + 1) * depth]


def stage_kernel(gate_ref, up_ref, gate_out_ref, up_out_ref):
    gate_out_ref[...] = gate_ref[...]
    up_out_ref[...] = up_ref[...]


def forward_kernel(tokens_ref, gate_ref, up_ref, _, out_ref):
    rows, part, depth = tokens_ref.shape
    hidden = gate_ref.shape[1]
    tokens = tokens_ref[...].reshape(rows * part, depth)
    for i, weight_ref in enumerate((gate_ref, up_ref)):
        total = jnp.dot(tokens, weight_ref[...], preferred_element_type=F32).astype(BF16)
        for row in range(rows):
            side, m = divmod(row, GROUP)
            out_ref[m, side * part : (side + 1) * part, i * hidden : (i + 1) * hidden] = total[
                row * part : (row + 1) * part
            ]


def sum_kernel(parts_ref, keep_ref, send_ref):
    total = parts_ref[0].astype(F32)
    for part in range(1, parts_ref.shape[0]):
        total += parts_ref[part].astype(F32)
    keep_ref[...] = total
    send_ref[...] = total.astype(BF16)


def act_kernel(where_ref, keep_ref, came_ref, cot_ref, far_cot_ref, out_ref):
    part = keep_ref.shape[0] // 2
    hidden = cot_ref.shape[1]
    half = rows_at(where_ref[1], part)
    for side, ref in ((where_ref[0], cot_ref), (1 - where_ref[0], far_cot_ref)):
        at = rows_at(side, part)
        cot = ref[half, :].astype(F32)
        total = keep_ref[at, :] + came_ref[at, :].astype(F32)
        gate, up = total[:, :hidden], total[:, hidden:]
        sig = 1.0 / (1.0 + jnp.exp(-gate))
        d_gate = (cot * up * sig * (1.0 + gate * (1.0 - sig))).astype(BF16)
        d_up = (cot * gate * sig).astype(BF16)
        for m in range(out_ref.shape[0]):
            out_ref[m, at, :hidden] = d_gate
            out_ref[m, at, hidden:] = d_up


def by_row(d_ref):
    part = d_ref.shape[1] // 2
    return jnp.concatenate(
        [
            d_ref[m, side * part : (side + 1) * part, :]
            for side in range(2)
            for m in range(GROUP)
        ],
        axis=0,
    )


def over_hidden(left, right):
    return lax.dot_general(left, right, (((1,), (1,)), ((), ())), preferred_element_type=F32)


def over_tokens(left, right):
    return lax.dot_general(left, right, (((0,), (0,)), ((), ())), preferred_element_type=F32)


def term_of(d_ref, gate_ref, up_ref):
    hidden = gate_ref.shape[1]
    d = by_row(d_ref)
    return over_hidden(d[:, :hidden], gate_ref[...]) + over_hidden(d[:, hidden:], up_ref[...])


def far_term_kernel(d_ref, gate_ref, up_ref, out_ref):
    out_ref[...] = term_of(d_ref, gate_ref, up_ref).astype(BF16)


def by_z_hi(rows):
    return [2 * y + z_hi for z_hi in range(2) for y in range(rows // 2)]


def near_term_kernel(d_ref, gate_ref, up_ref, came_ref, out_ref):
    rows, part, _ = out_ref.shape
    total = (term_of(d_ref, gate_ref, up_ref) + came_ref[...].astype(F32)).astype(BF16)
    for i, row in enumerate(by_z_hi(rows)):
        out_ref[i] = total[row * part : (row + 1) * part]


def weight_grad_kernel(far_ref, near_ref, d_far_ref, d_near_ref, gate_ref, up_ref):
    rows, part, depth = far_ref.shape
    hidden = gate_ref.shape[1]
    far = far_ref[...].reshape(rows * part, depth)
    near = near_ref[...].reshape(rows * part, depth)
    d_far, d_near = by_row(d_far_ref), by_row(d_near_ref)
    for i, ref in enumerate((gate_ref, up_ref)):
        span = slice(i * hidden, (i + 1) * hidden)
        total = over_tokens(far, d_far[:, span]) + over_tokens(near, d_near[:, span])
        ref[...] = total.astype(BF16)


def call(kernel, outs, n_where, n_in, flops=0, nbytes=0, n_any=0):
    return pl.pallas_call(
        kernel,
        out_shape=outs,
        in_specs=[SMEM] * n_where + [VMEM] * n_in + [ANY] * n_any,
        out_specs=jax.tree.map(lambda _: VMEM, outs),
        compiler_params=pltpu.CompilerParams(vmem_limit_bytes=VMEM_BYTES),
        cost_estimate=pl.CostEstimate(flops=flops, bytes_accessed=nbytes, transcendentals=0),
    )


def shards(rows, cols, inputs, cotangent, gate_weight, up_weight):
    depth, hidden = gate_weight.shape
    part = inputs.shape[0] // 2
    wide = 2 * hidden
    flops = 2 * rows * part * depth * wide
    pairs = [list(range(0, GROUP)), list(range(GROUP, 2 * GROUP))]
    core_groups = [[2 * r + core for r in by_z_hi(rows)] for core in range(2)]
    row, col = lax.axis_index("row"), lax.axis_index("col")

    def scalar(value):
        return value.astype(jnp.int32).reshape(1)

    side = scalar(row // GROUP)
    halves = {"far": scalar(1 - col % 2), "near": scalar(col % 2)}

    def shape(dims, dtype=BF16):
        return jax.ShapeDtypeStruct(dims, dtype)

    def exchange(array, axis, groups=None):
        return lax.all_to_all(array, axis, 0, 0, axis_index_groups=groups)

    def swap(array, axis, count, bit):
        return lax.ppermute(array, axis, [(i, i ^ bit) for i in range(count)])

    sent = call(lay_kernel, shape((rows, part, depth)), 1, 1)(halves["far"], inputs)
    tokens = {"far": exchange(sent, "row")}
    tokens["near"] = swap(tokens["far"], "col", cols, 1)

    grad = shape((depth, hidden))
    gate, up = call(stage_kernel, [grad, grad], 0, 2, nbytes=8 * depth * hidden)(
        gate_weight, up_weight
    )
    far_cot = swap(cotangent, "row", rows, GROUP)
    d = {}
    for half in ("far", "near"):
        partial = call(forward_kernel, shape((GROUP, 2 * part, wide)), 0, 3, flops, n_any=1)(
            tokens[half], gate, up, far_cot if half == "near" else side
        )
        parts = exchange(partial, "row", pairs)
        keep, send = call(
            sum_kernel, [shape((2 * part, wide), F32), shape((2 * part, wide))], 0, 1
        )(parts)
        came = swap(send, "row", rows, GROUP)
        copies = call(act_kernel, shape((GROUP, 2 * part, wide)), 1, 4)(
            jnp.concatenate([side, halves[half]]), keep, came, cotangent, far_cot
        )
        d[half] = exchange(copies, "row", pairs)

    far_term = call(far_term_kernel, shape((rows * part, depth)), 0, 3, flops)(
        d["far"], gate, up
    )
    came = swap(far_term, "col", cols, 1)
    term = call(near_term_kernel, shape((rows, part, depth)), 0, 4, flops)(
        d["near"], gate, up, came
    )
    over_col = exchange(term, "col", core_groups)
    input_grad = jnp.sum(over_col.astype(F32), axis=0).astype(BF16)

    gate_grad, up_grad = call(weight_grad_kernel, [grad, grad], 0, 4, 2 * flops)(
        tokens["far"], tokens["near"], d["far"], d["near"]
    )
    return (input_grad, gate_grad, up_grad)


def solution(mesh):
    in_specs = (P("row", None), P("row", "col"), P("row", "col"), P("row", "col"))
    out_specs = (P("col", "row"), P("row", "col"), P("row", "col"))
    local = functools.partial(shards, mesh.shape["row"], mesh.shape["col"])
    return jax.shard_map(local, mesh=mesh, in_specs=in_specs, out_specs=out_specs, check_vma=False)
```
